256 devices in a mesh: rows: 128 (over z, x, y), rep: 2 (over core).
Axes of the slice: x: 4, y: 4, z: 8, core: 2. Of those that a mesh axis runs over, the one named last changes fastest.
Arguments:
- features: bfloat16 [196608, 256], P('rows'), may hold values from -6 to 6
- degrees: int32 [196608], P('rows'), may hold values from 32 to 512
- weight: bfloat16 [256, 256], replicated, may hold values from -0.375 to 0.375
- tile_values: bfloat16 [128, 8, 22, 256, 256], P('rows', None, 'rep'), may hold values from 0.25 to 4
- tile_pos: int32 [128, 8, 22], P('rows'), may hold values from 0 to 35, as said below
- live: int32 [128, 8], P('rows'), may hold values from 1 to 22, as said below
Outputs:
- updated: bfloat16 [196608, 256], P('rows')
The draws below stay inside these ranges and needn't reach their ends.
Inputs may be any that keep to these rules, and one draw needn't show every extreme that they name: `tile_pos`: within one row block and one column block the 22 positions are distinct. `live`: some row block has 22 used slots in every column block.
All inputs are finite; a program needn't handle non-finite values.
Results may differ from the reference program's by a relative error of at most 0.0052.
Values may be sent and summed in bfloat16 or wider, within the bound.
No kernel may reach another device: no remote copies, remote signals or barrier semaphores. Data moves between devices by JAX's collectives and lax.ppermute only.
A program may use at most 128 MiB of HBM per device.

```python
import math
import jax
import jax.numpy as jnp
from jax import lax

F = 256
TILE = 256
FB = 1536
MAXT = 22
KT = 6
COLBLOCKS = 8
ROWBLOCKS = 128
NODES = 196608
N_ROWS = 128


def draw_tile_pos(key, part):
    key = jax.random.fold_in(key, 11)
    keys = jax.random.split(key, ROWBLOCKS * COLBLOCKS)
    orders = jax.vmap(lambda single: jax.random.permutation(single, KT * KT))(keys)
    return orders[:, :MAXT].reshape(ROWBLOCKS, COLBLOCKS, MAXT).astype(jnp.int32)


def draw_live(key, part):
    key = jax.random.fold_in(key, 23)
    first, second, third = jax.random.split(key, 3)
    base = jax.random.randint(first, (ROWBLOCKS, COLBLOCKS), 1, MAXT // 2 + 1)
    busy = jax.random.randint(second, (ROWBLOCKS, 1), 0, 4) == 0
    chosen = jax.random.randint(third, (), 0, ROWBLOCKS)
    fullrow = jnp.arange(ROWBLOCKS)[:, None] == chosen
    return jnp.where(busy | fullrow, MAXT, base).astype(jnp.int32)


def touch_ends(entries, stream_key, smallest, high):
    place = [jax.random.randint(jax.random.fold_in(stream_key, axis), (), 0, length) for axis, length in enumerate(entries.shape)]
    widest = entries.shape.index(max(entries.shape))
    next_to = place[:widest] + [(place[widest] + 1) % entries.shape[widest]] + place[widest + 1:]
    return entries.at[tuple(place)].set(smallest).at[tuple(next_to)].set(high)


def block_levels(rng, dims, cuts, smallest, high):
    level, own = 1.0, jax.random.fold_in(rng, 6)
    for position, shards_of in cuts:
        steps = jnp.exp(jax.random.uniform(jax.random.fold_in(own, position), (shards_of,), jnp.float32, smallest / len(cuts), high / len(cuts)))
        level = level * jnp.repeat(steps, dims[position] // shards_of).reshape([-1 if axis == position else 1 for axis in range(len(dims))])
    return level


def bell_draw(stream_key, extent, width, reach, cuts=(), kind=jnp.bfloat16):
    gain = block_levels(stream_key, extent, cuts, -0.22, 0.18) if cuts else 1.0
    values = jax.random.normal(stream_key, extent, jnp.float32) * width * gain
    return jnp.minimum(jnp.maximum(values, -reach), reach).astype(kind)


def setup_inputs(seed: int = 0) -> dict:
    splits = jax.random.split(jax.random.key(seed), 7)
    features = bell_draw(splits[0], (NODES, F), 1.0, 6.0, ((0, 128),))
    degrees = touch_ends(jax.random.randint(splits[1], (NODES,), 32, 513), jax.random.fold_in(splits[1], 1), 32, 512).astype(jnp.int32)
    weight = bell_draw(splits[2], (F, F), F ** -0.5, 0.375)
    tile_values = jnp.clip(jnp.exp(math.log(4.0) - 2.7725887 * jax.random.uniform(splits[3], (ROWBLOCKS, COLBLOCKS, MAXT, TILE, TILE), jnp.float32) ** block_levels(splits[3], (ROWBLOCKS, COLBLOCKS, MAXT, TILE, TILE), ((0, 128), (2, 2)), -0.2, 0.2)), 0.25, 4.0).astype(jnp.bfloat16)
    tile_pos = draw_tile_pos(jax.random.fold_in(splits[6], 71), 0)
    live = draw_live(jax.random.fold_in(splits[6], 71), 0)
    return {"features": features, "degrees": degrees, "weight": weight, "tile_values": tile_values, "tile_pos": tile_pos, "live": live}


def reference(features, degrees, weight, tile_values, tile_pos, live):
    inverse = lax.rsqrt(degrees.astype(jnp.float32))
    scaled = (features.astype(jnp.float32) * inverse[:, None]).astype(jnp.bfloat16)
    side = FB // TILE
    stride = N_ROWS // COLBLOCKS
    sources = scaled.reshape(N_ROWS, side, TILE, F)[jnp.arange(COLBLOCKS) * stride].astype(jnp.float32)

    def one_block(index):
        tiles = tile_values[index].astype(jnp.float32)
        places = tile_pos[index]
        pieces = sources[jnp.arange(COLBLOCKS)[:, None], places % side]
        product = jnp.einsum('gmab,gmbf->gmaf', tiles, pieces, precision=lax.Precision.HIGHEST)
        active = (jnp.arange(MAXT)[None, :] < live[index][:, None]).astype(jnp.float32)
        target = ((places // side)[..., None] == jnp.arange(side)).astype(jnp.float32) * active[..., None]
        summed = jnp.einsum('gmk,gmaf->kaf', target, product, precision=lax.Precision.HIGHEST)
        return summed.reshape(FB, F)
    total = lax.map(one_block, jnp.arange(N_ROWS)).reshape(NODES, F)
    combined = (total * inverse[:, None] + features.astype(jnp.float32)).astype(jnp.bfloat16)
    result = jnp.dot(combined, weight, preferred_element_type=jnp.float32)
    return jax.nn.relu(result).astype(jnp.bfloat16)
```

```python
import functools
import itertools

import jax
import jax.numpy as jnp
import numpy as np
from jax import lax
from jax.experimental import pallas as pl
from jax.experimental.pallas import tpu as pltpu
from jax.sharding import PartitionSpec as P

NZ, NX, NY, CORES = 8, 4, 4, 2
COLORS = 4
AXES = ("rows", "rep")
CHIPS = list(itertools.product(range(NZ), range(NX), range(NY)))
FIRST_HEIGHTS = (0, 2, 5, 7)


def flat(z, x, y, core):
    return ((z % NZ * NX + x % NX) * NY + y % NY) * CORES + core


def color_of(z, x, y):
    return (z + 2 * x - y) % COLORS


def place_of(color, height, x):
    return (height + color) % NZ, x % NX, (height + 2 * x) % NY


def plan():
    scatter = [[] for _ in range(3)]
    spread = [[] for _ in range(3)]
    gather = [[] for _ in range(7)]
    trade = [[] for _ in range(3)]
    for color, core in itertools.product(range(COLORS), range(CORES)):
        at = lambda height, x: flat(*place_of(color, height, x), core)
        for base in (0, 4):
            for i in range(1, 4):
                scatter[i - 1].append((at(base, 0), at(base, i)))
            for x in range(NX):
                for i, height in enumerate(FIRST_HEIGHTS[1:]):
                    spread[i].append((at(base, x), at(base + height, x)))
        for height, x in itertools.product(range(NZ), range(NX)):
            for i in range(1, 8):
                other = height ^ (i // 4)
                gather[i - 1].append((at(other, x + i % 4), at(height, x)))
    for z, x, y in CHIPS:
        for core in range(CORES):
            s = 1 if core == 0 else -1
            for i, (dz, dx, dy) in enumerate(((1, 0, 0), (0, 1, 0), (0, 0, 1))):
                trade[i].append((flat(z, x, y, core), flat(z + s * dz, x + s * dx, y + s * dy, core)))
    return scatter, spread, gather, trade


def facts():
    rows = []
    for z, x, y in CHIPS:
        color = color_of(z, x, y)
        height = (z - color) % NZ
        slot = lambda h, i: (0 if h % NZ in FIRST_HEIGHTS else 4) + i % NX
        for core in range(CORES):
            s = 1 if core == 0 else -1
            row = [int(x == 0 and y == 0)]
            row += [slot(height ^ (i // 4), x + i % 4) for i in range(8)]
            row += [color, (color - s) % COLORS, (color - 2 * s) % COLORS, (color + s) % COLORS]
            rows.append(row)
    return np.array(rows, np.int32)


def assemble_kernel(slots, *refs):
    *pieces, out = refs
    size = pieces[0].shape[0]
    for i, piece in enumerate(pieces):
        out[pl.ds(pl.multiple_of(slots[i] * size, size), size), :] = piece[...]


def multiply_kernel(first, last, which, table, own, peer, payload, *refs):
    if last:
        inverse, features, *refs = refs
    if first:
        out, *refs = refs
        acc = out
    elif last:
        before, out, *refs = refs
        acc = refs.pop(0)
    else:
        before, out, *refs = refs
        acc = out
    buffer, sems = refs
    blocks = own.shape[0]
    half = own.shape[1]
    tile = own.shape[2]
    height = payload.shape[0] // 2
    copies = []
    for i in range(2):
        block = which[0] + i * COLORS
        for j, source in enumerate((own, peer)):
            copy = pltpu.make_async_copy(source.at[block], buffer.at[i, j], sems.at[i, j])
            copy.start()
            copies.append((i, j, block, copy))
    acc[...] = jnp.zeros_like(acc) if first else before[...]
    for i, j, block, copy in copies:
        copy.wait()
        for k in range(half):
            entry = (block * 2 + j) * half + k
            row = pl.multiple_of(table[entry], tile)
            column = pl.multiple_of(table[2 * blocks * half + entry] + i * height, tile)
            acc[pl.ds(row, tile), :] += jnp.dot(
                buffer[i, j, k], payload[pl.ds(column, tile), :], preferred_element_type=jnp.float32
            )
    if last:
        total = acc[pl.ds(0, height), :]
        out[...] = (total * inverse[...] + features[...].astype(jnp.float32)).astype(out.dtype)


def multiply(which, table, own, peer, payload, before=None, inverse=None, features=None):
    first, last = before is None, inverse is not None
    blocks, half, tile, _ = own.shape
    height, width = payload.shape[0] // 2, payload.shape[1]
    acc = jax.ShapeDtypeStruct((height + tile, width), jnp.float32)
    vmem = pl.BlockSpec(memory_space=pltpu.VMEM)
    smem = pl.BlockSpec(memory_space=pltpu.SMEM)
    hbm = pl.BlockSpec(memory_space=pl.ANY)
    args = [which, table, own, peer, payload]
    specs = [smem, smem, hbm, hbm, vmem]
    if last:
        args += [inverse, features]
        specs += [vmem, vmem]
    alias = {}
    if not first:
        args.append(before)
        specs.append(vmem)
        if not last:
            alias = {len(args) - 1: 0}
    scratch = [pltpu.VMEM(acc.shape, acc.dtype)] if last else []
    scratch += [pltpu.VMEM((2, 2, half, tile, tile), own.dtype), pltpu.SemaphoreType.DMA((2, 2))]
    return pl.pallas_call(
        functools.partial(multiply_kernel, first, last),
        out_shape=jax.ShapeDtypeStruct((height, width), payload.dtype) if last else acc,
        in_specs=specs,
        out_specs=vmem,
        scratch_shapes=scratch,
        input_output_aliases=alias,
        compiler_params=pltpu.CompilerParams(vmem_limit_bytes=24 * 2**20),
        cost_estimate=pl.CostEstimate(
            flops=4 * half * 2 * tile * tile * 256, bytes_accessed=4 * half * tile * tile * 2, transcendentals=0
        ),
    )(*args)


def finish_kernel(mine, other, mine_weight, other_weight, out):
    here = jnp.dot(mine[...], mine_weight[...], preferred_element_type=jnp.float32)
    there = jnp.dot(other[...], other_weight[...], preferred_element_type=jnp.float32)
    out[...] = jnp.maximum(here + there, 0.0).astype(out.dtype)


def on_device(features, degrees, weight, tile_values, tile_pos, live):
    scatter, spread, gather, trade = plan()
    swap = [(i, i ^ 1) for i in range(len(CHIPS) * CORES)]
    send = lambda x, pairs: lax.ppermute(x, AXES, pairs)
    height, full = features.shape
    width = full // CORES
    blocks, half, tile = tile_values.shape[1:4]
    side = height // tile
    core = lax.axis_index("rep")
    me = lax.axis_index("rows") * CORES + core
    fact = lax.dynamic_index_in_dim(jnp.asarray(facts()), me, 0, keepdims=False)

    own = tile_values[0]
    peer = send(own, swap)

    inverse = lax.rsqrt(degrees.astype(jnp.float32))
    mine = lax.dynamic_slice_in_dim(features, core * width, width, 1)
    scaled = (mine.astype(jnp.float32) * inverse[:, None]).astype(jnp.bfloat16)

    quarter = scaled.reshape(4, height // 4, width)
    piece = jnp.where(fact[0] == 1, quarter[0], jnp.zeros_like(quarter[0]))
    for got in [send(quarter[i + 1], pairs) for i, pairs in enumerate(scatter)]:
        piece = piece + got
    kept = piece
    for got in [send(kept, pairs) for pairs in spread]:
        piece = piece + got
    pieces = [piece] + [send(piece, pairs) for pairs in gather]
    vmem = pl.BlockSpec(memory_space=pltpu.VMEM)
    smem = pl.BlockSpec(memory_space=pltpu.SMEM)
    payload = pl.pallas_call(
        assemble_kernel,
        out_shape=jax.ShapeDtypeStruct((8 * height // 4, width), scaled.dtype),
        in_specs=[smem] + [vmem] * 8,
        out_specs=vmem,
    )(fact[1:9], *pieces)
    arrived = [payload] + [send(payload, pairs) for pairs in trade]

    used = jnp.arange(half * CORES)[None, :] < live[0][:, None]
    row = jnp.where(used, tile_pos[0] // side, side) * tile
    column = tile_pos[0] % side * tile
    both = jnp.stack([row, column]).reshape(2, blocks, CORES, half)
    table = jnp.where(core == 0, both, both[:, :, ::-1]).reshape(-1)
    spread_inverse = jnp.broadcast_to(inverse[:, None], (height, width))

    acc = multiply(fact[9:10], table, own, peer, arrived[0])
    for i in (1, 2):
        acc = multiply(fact[9 + i : 10 + i], table, own, peer, arrived[i], acc)
    combined = multiply(fact[12:13], table, own, peer, arrived[3], acc, spread_inverse, mine)

    other = send(combined, swap)
    mine_weight = lax.dynamic_slice_in_dim(weight, core * width, width, 0)
    other_weight = lax.dynamic_slice_in_dim(weight, (1 - core) * width, width, 0)
    return pl.pallas_call(
        finish_kernel,
        out_shape=jax.ShapeDtypeStruct((height, full), jnp.bfloat16),
        in_specs=[vmem] * 4,
        out_specs=vmem,
    )(combined, other, mine_weight, other_weight)


def solution(mesh):
    placed = (
        P("rows", None),
        P("rows"),
        P(),
        P("rows", None, "rep", None, None),
        P("rows", None, None),
        P("rows", None),
    )
    return jax.shard_map(on_device, mesh=mesh, in_specs=placed, out_specs=P("rows", None), check_vma=False)
```

```python
import functools
import itertools

import jax
import jax.numpy as jnp
import numpy as np
from jax import lax
from jax.experimental import pallas as pl
from jax.experimental.pallas import tpu as pltpu
from jax.sharding import PartitionSpec as P

NZ, NX, NY, CORES = 8, 4, 4, 2
AXES = ("rows", "rep")
CHIPS = list(itertools.product(range(NZ), range(NX), range(NY)))
COLORS = 4
FIRST_PIECE = ((0, 0), (0, 3), (2, 0), (2, 3), (5, 0), (5, 3), (7, 0), (7, 3))
SECOND_PIECE = ((1, 1), (0, 2), (2, 1), (2, 2), (4, 1), (5, 2), (7, 1), (7, 2))
SEEDS = ((7, 0), (0, 2), (1, 1))
CHILDREN = {
    (0, 0): ((2, 3), (7, 3), (0, 3)),
    (7, 0): ((5, 3), (5, 0), (2, 0)),
    (0, 2): ((7, 2), (2, 1), (5, 2)),
    (1, 1): ((7, 1), (4, 1), (2, 2)),
}


def flat(z, x, y, core):
    return ((z % NZ * NX + x % NX) * NY + y % NY) * CORES + core


def color_of(z, x, y, core):
    return (z + 2 * x - y if core == 0 else z + 2 * y - x) % COLORS


def chip_at(color, height, across, core):
    other = height % NZ + 2 * across
    return ((color + height) % NZ, across, other) if core == 0 else ((color + height) % NZ, other, across)


def slot_of(height, across):
    for base in (0, 4):
        place = ((height - base) % NZ, across)
        for piece, places in enumerate((FIRST_PIECE, SECOND_PIECE)):
            if place in places:
                return base // 2 + piece


def plan():
    scatter, spread, gather, trade = ([[] for _ in range(3)] for _ in range(4))
    for color, core in itertools.product(range(COLORS), range(CORES)):
        at = lambda height, across: flat(*chip_at(color, height, across, core), core)
        for base in (0, 4):
            for i, (height, across) in enumerate(SEEDS):
                scatter[i].append((at(base, 0), at(base + height, across)))
            for (height, across), places in CHILDREN.items():
                for i, (h, a) in enumerate(places):
                    spread[i].append((at(base + height, across), at(base + h, a)))
        for height, across in itertools.product(range(NZ), range(NX)):
            for i in range(1, 4):
                gather[i - 1].append((at(height ^ (i & 1), across ^ (i >> 1)), at(height, across)))
    for z, x, y in CHIPS:
        for core, s in ((0, 1), (1, -1)):
            for i, (dz, dx, dy) in enumerate(((1, 0, 0), (0, 1, 0), (0, 0, 1))):
                trade[i].append((flat(z, x, y, core), flat(z + s * dz, x + s * dx, y + s * dy, core)))
    return scatter, spread, gather, trade


def facts():
    rows = []
    for z, x, y in CHIPS:
        for core, s in ((0, 1), (1, -1)):
            color = color_of(z, x, y, core)
            height, across = (z - color) % NZ, (x, y)[core]
            row = [int(x == 0 and y == 0)]
            row += [slot_of(height ^ (i & 1), across ^ (i >> 1)) for i in range(4)]
            sent = [color_of(z - s, x, y, core), color_of(z, x - s, y, core), color_of(z, x, y - s, core)]
            row += [color, color + COLORS] + sent + [c + COLORS for c in sent]
            rows.append(row)
    return np.array(rows, np.int32)


VMEM = pl.BlockSpec(memory_space=pltpu.VMEM)
SMEM = pl.BlockSpec(memory_space=pltpu.SMEM)
HBM = pl.BlockSpec(memory_space=pltpu.HBM)


def assemble_kernel(slots, *refs):
    *pieces, first, second = refs
    size = pieces[0].shape[0]
    for i, piece in enumerate(pieces):
        place = pl.ds(pl.multiple_of(slots[i] % 2 * size, size), size)

        @pl.when(slots[i] < 2)
        def _():
            first[place, :] = piece[...]

        @pl.when(slots[i] >= 2)
        def _():
            second[place, :] = piece[...]


def prepare_kernel(order, table, own, peer, *refs):
    *mats, done, sems = refs
    blocks, half, tile = own.shape[:3]
    slots = CORES * half

    def place(j, k, act):
        entry = order[j] * slots + k
        row, column = table[entry], table[blocks * slots + entry]

        @pl.when(row >= 0)
        def _():
            target = mats[j].at[pl.ds(pl.multiple_of(row, tile), tile), pl.ds(pl.multiple_of(column, tile), tile)]
            act(pltpu.make_async_copy((own if k < half else peer).at[order[j], k % half], target, sems.at[j]))

    for j in range(blocks):
        mats[j][...] = jnp.zeros(mats[j].shape, mats[j].dtype)
        for k in range(slots):
            place(j, k, lambda copy: copy.start())
    for j in range(blocks):
        for k in range(slots):
            place(j, k, lambda copy: copy.wait())
    done[...] = jnp.zeros_like(done)


def multiply_kernel(first, last, mat, source, *refs):
    product = jnp.dot(mat[...], source[...], preferred_element_type=jnp.float32)
    if not first:
        before, *refs = refs
        product = before[...] + product
    if last:
        inverse, features, out = refs
        out[...] = (product * inverse[...] + features[...].astype(jnp.float32)).astype(out.dtype)
    else:
        refs[0][...] = product


def multiply(mat, source, before=None, extra=()):
    first, last = before is None, bool(extra)
    args = [mat, source] + ([] if first else [before]) + list(extra)
    return pl.pallas_call(
        functools.partial(multiply_kernel, first, last),
        out_shape=jax.ShapeDtypeStruct(source.shape, source.dtype if last else jnp.float32),
        in_specs=[VMEM] * len(args),
        out_specs=VMEM,
        input_output_aliases={} if first or last else {2: 0},
        compiler_params=pltpu.CompilerParams(vmem_limit_bytes=6 * 2**20),
        cost_estimate=pl.CostEstimate(
            flops=4 * mat.size * source.shape[1], bytes_accessed=mat.size * 2, transcendentals=0
        ),
    )(*args)


def finish_kernel(mine, other, mine_weight, other_weight, out):
    here = jnp.dot(mine[...], mine_weight[...], preferred_element_type=jnp.float32)
    there = jnp.dot(other[...], other_weight[...], preferred_element_type=jnp.float32)
    out[...] = jnp.maximum(here + there, 0.0).astype(out.dtype)


def on_device(features, degrees, weight, tile_values, tile_pos, live):
    scatter, spread, gather, trade = plan()
    swap = [(i, i ^ 1) for i in range(len(CHIPS) * CORES)]
    send = lambda x, pairs: lax.ppermute(x, AXES, pairs)
    height, full = features.shape
    width = full // CORES
    blocks, half, tile = tile_values.shape[1:4]
    side = height // tile
    core = lax.axis_index("rep")
    me = lax.axis_index("rows") * CORES + core
    fact = lax.dynamic_index_in_dim(jnp.asarray(facts()), me, 0, keepdims=False)
    order = fact[5:]

    own = tile_values[0]
    peer = send(own, swap)

    inverse = lax.rsqrt(degrees.astype(jnp.float32))
    mine = lax.dynamic_slice_in_dim(features, core * width, width, 1)
    scaled = (mine.astype(jnp.float32) * inverse[:, None]).astype(jnp.bfloat16)

    used = jnp.arange(half * CORES)[None, :] < live[0][:, None]
    row = jnp.where(used, tile_pos[0] // side * tile, -1)
    column = tile_pos[0] % side * tile
    both = jnp.stack([row, column]).reshape(2, blocks, CORES, half)
    table = jnp.where(core == 0, both, both[:, :, ::-1]).reshape(-1)

    cut = scaled.reshape(2, height // 2, width)
    piece = jnp.where(fact[0] == 1, cut[0], jnp.zeros_like(cut[0]))
    for got in [send(cut[min(i, 1)], pairs) for i, pairs in enumerate(scatter)]:
        piece = piece + got
    kept = piece
    table, kept = lax.optimization_barrier((table, kept))
    matrix = jax.ShapeDtypeStruct((height, height), own.dtype)
    *mats, done = pl.pallas_call(
        prepare_kernel,
        out_shape=[matrix] * blocks + [jax.ShapeDtypeStruct((16, width), own.dtype)],
        in_specs=[SMEM, SMEM, HBM, HBM],
        out_specs=[VMEM] * (blocks + 1),
        scratch_shapes=[pltpu.SemaphoreType.DMA((blocks,))],
        compiler_params=pltpu.CompilerParams(vmem_limit_bytes=42 * 2**20),
        cost_estimate=pl.CostEstimate(flops=0, bytes_accessed=4 * own.size * 2, transcendentals=0),
    )(order, table, own, peer)
    for got in [send(kept, pairs) for pairs in spread]:
        piece = piece + got
    piece = piece + done[:1]
    pieces = [piece] + [send(piece, pairs) for pairs in gather]
    half_block = jax.ShapeDtypeStruct((height, width), scaled.dtype)
    first, second = pl.pallas_call(
        assemble_kernel,
        out_shape=(half_block, half_block),
        in_specs=[SMEM] + [VMEM] * 4,
        out_specs=(VMEM, VMEM),
        compiler_params=pltpu.CompilerParams(vmem_limit_bytes=4 * 2**20),
    )(fact[1:5], *pieces)
    arrived = [send(block, pairs) for block in (first, second) for pairs in trade]

    spread_inverse = jnp.broadcast_to(inverse[:, None], (height, width))
    total = None
    for i, source in enumerate([first, second] + arrived):
        total = multiply(mats[i], source, total, (spread_inverse, mine) if i == blocks - 1 else ())
    combined = total

    other = send(combined, swap)
    mine_weight = lax.dynamic_slice_in_dim(weight, core * width, width, 0)
    other_weight = lax.dynamic_slice_in_dim(weight, (1 - core) * width, width, 0)
    return pl.pallas_call(
        finish_kernel,
        out_shape=jax.ShapeDtypeStruct((height, full), jnp.bfloat16),
        in_specs=[VMEM] * 4,
        out_specs=VMEM,
        compiler_params=pltpu.CompilerParams(vmem_limit_bytes=6 * 2**20),
    )(combined, other, mine_weight, other_weight)


def solution(mesh):
    placed = (
        P("rows", None),
        P("rows"),
        P(),
        P("rows", None, "rep", None, None),
        P("rows", None, None),
        P("rows", None),
    )
    return jax.shard_map(on_device, mesh=mesh, in_specs=placed, out_specs=P("rows", None), check_vma=False)
```

```python
import functools
import itertools

import jax
import jax.numpy as jnp
import numpy as np
from jax import lax
from jax.experimental import pallas as pl
from jax.experimental.pallas import tpu as pltpu
from jax.sharding import PartitionSpec as P

NZ, NX, NY, CORES = 8, 4, 4, 2
AXES = ("rows", "rep")
CHIPS = list(itertools.product(range(NZ), range(NX), range(NY)))
COLORS = 4
PIECES = 4
SIGNS = ((1, 1), (1, -1), (-1, 1), (-1, -1))
HOLDERS = (
    ((0, 0), (2, 1), (0, 3), (6, 1), (1, 3), (3, 0), (6, 3), (4, 3)),
    ((0, 2), (3, 2), (5, 2), (1, 1), (0, 1), (4, 1), (5, 1), (2, 2)),
    ((7, 3), (5, 0), (7, 1), (6, 2), (2, 3), (2, 0), (4, 2), (4, 0)),
    ((7, 0), (7, 2), (6, 0), (5, 3), (1, 0), (3, 1), (3, 3), (1, 2)),
)
GROUP_SHIFT = 1
PARTNERS = 1


def flat(z, x, y, core):
    return ((z % NZ * NX + x % NX) * NY + y % NY) * CORES + core


def color_of(z, x, y, core):
    return (z + 2 * x - y if core == 0 else z + 2 * y - x) % COLORS


def chip_at(color, height, across, core):
    up, side = SIGNS[color]
    height, across = up * height % NZ, side * across % NX
    z, other = color + COLORS * core + height, height + 2 * across
    return (z, across, other) if core == 0 else (z, other, across)


def partner(height, across, i):
    if i & 1:
        height = (height - GROUP_SHIFT ^ 1) + GROUP_SHIFT
    return height % NZ, across ^ (PARTNERS if i & 2 else 0)


def plan():
    scatter = [[] for _ in range(PIECES)]
    spread, gather, trade = ([[] for _ in range(3)] for _ in range(3))
    for color, core in itertools.product(range(COLORS), range(CORES)):
        at = lambda place, on=core: flat(*chip_at(color, *place, core), on)
        owner = (0, 0)
        for piece, places in enumerate(HOLDERS):
            if places[0] != owner:
                scatter[piece].append((at(owner), at(places[0])))
                scatter[piece].append((at(owner, 1 - core), at(places[4])))
            else:
                scatter[piece].append((at(owner), at(places[4])))
            for holder in (0, 4):
                for i in range(3):
                    spread[i].append((at(places[holder]), at(places[holder + 1 + i])))
        for place in itertools.product(range(NZ), range(NX)):
            for i in range(1, 4):
                gather[i - 1].append((at(partner(*place, i)), at(place)))
    for z, x, y in CHIPS:
        for core, s in ((0, 1), (1, -1)):
            for i, (dz, dx, dy) in enumerate(((1, 0, 0), (0, 1, 0), (0, 0, 1))):
                trade[i].append((flat(z, x, y, core), flat(z + s * dz, x + s * dx, y + s * dy, core)))
    return scatter, spread, gather, trade


def facts():
    rows = []
    for z, x, y in CHIPS:
        for core, s in ((0, 1), (1, -1)):
            color = color_of(z, x, y, core)
            up, side = SIGNS[color]
            place = up * (z - color - COLORS * core) % NZ, side * (x, y)[core] % NX
            row = [int(place == (0, 0))]
            for i in range(4):
                row.append(next(p for p, places in enumerate(HOLDERS) if partner(*place, i) in places))
            sent = [color_of(z - s, x, y, core), color_of(z, x - s, y, core), color_of(z, x, y - s, core)]
            row += [c + COLORS * core for c in [color] + sent]
            rows.append(row)
    return np.array(rows, np.int32)


VMEM = pl.BlockSpec(memory_space=pltpu.VMEM)
SMEM = pl.BlockSpec(memory_space=pltpu.SMEM)
HBM = pl.BlockSpec(memory_space=pltpu.HBM)


def inverse_columns(degrees):
    groups, lanes = degrees.shape
    padded = jnp.concatenate([degrees[...], jnp.ones((-groups % 8, lanes), degrees.dtype)], axis=0)
    return lax.rsqrt(padded.astype(jnp.float32)).T


def scale_kernel(blocks, features, degrees, *refs):
    *outs, held, held_degrees, sems = refs

    @pl.when(lax.axis_index("rows") % (lax.axis_size("rows") // blocks) == 0)
    def _():
        copies = [
            pltpu.make_async_copy(degrees, held_degrees, sems.at[0]),
            pltpu.make_async_copy(features, held, sems.at[1]),
        ]
        for copy in copies:
            copy.start()
        copies[0].wait()
        inverse = inverse_columns(held_degrees)
        copies[1].wait()
        groups, size = degrees.shape
        for i in range(groups):
            out, place = outs[i * len(outs) // groups], i % (groups // len(outs)) * size
            here = held[pl.ds(i * size, size), :].astype(jnp.float32)
            out[pl.ds(place, size), :] = (here * inverse[:, i : i + 1]).astype(out.dtype)


def assemble_kernel(slots, *refs):
    *pieces, out = refs
    size = pieces[0].shape[0]
    for i, piece in enumerate(pieces):
        out[pl.ds(pl.multiple_of(slots[i] * size, size), size), :] = piece[...]


def prepare_kernel(order, table, own, peer, *refs):
    *mats, sems = refs
    blocks, half, tile = own.shape[:3]
    slots = CORES * half
    places = [(j, k) for j in range(len(mats)) for k in range(slots)]

    def place(j, k, act):
        entry = order[j] * slots + k
        row, column = table[entry], table[blocks * slots + entry]

        @pl.when(row >= 0)
        def _():
            target = mats[j].at[pl.ds(pl.multiple_of(row, tile), tile), pl.ds(pl.multiple_of(column, tile), tile)]
            act(pltpu.make_async_copy((own if k < half else peer).at[order[j], k % half], target, sems.at[j]))

    for j, k in places:
        if k == 0:
            mats[j][...] = jnp.zeros(mats[j].shape, mats[j].dtype)
        place(j, k, lambda copy: copy.start())
    for j, k in places:
        place(j, k, lambda copy: copy.wait())


def multiply_kernel(mat, source, *refs):
    *before, out = refs
    product = jnp.dot(mat[...], source[...], preferred_element_type=jnp.float32)
    out[...] = before[0][...] + product if before else product


def multiply_part_kernel(start, mat, source, before, out):
    rows = pl.ds(start, out.shape[0])
    out[...] = before[rows, :] + jnp.dot(mat[rows, :], source[...], preferred_element_type=jnp.float32)


def multiply(mat, source, before=None, part=None):
    args = [mat, source] + ([] if before is None else [before])
    height, width = source.shape
    if part is None:
        kernel, alias = multiply_kernel, ({} if before is None else {2: 0})
    else:
        height //= 2
        kernel, alias = functools.partial(multiply_part_kernel, part * height), {}
    return pl.pallas_call(
        kernel,
        out_shape=jax.ShapeDtypeStruct((height, width), jnp.float32),
        in_specs=[VMEM] * len(args),
        out_specs=VMEM,
        input_output_aliases=alias,
        compiler_params=pltpu.CompilerParams(vmem_limit_bytes=10 * 2**20),
        cost_estimate=pl.CostEstimate(
            flops=2 * height * mat.shape[1] * width, bytes_accessed=mat.size * 2, transcendentals=0
        ),
    )(*args)


def finish_kernel(start, mine, other, degrees, features, weight, *refs):
    *_, out, done, sem = refs
    rows = pl.ds(start, mine.shape[0])
    inverse = inverse_columns(degrees)
    size = degrees.shape[1]
    for i in range(mine.shape[0] // size):
        here = pl.ds(i * size, size)
        column = start // size + i
        total = (mine[here, :] + other[here, :]) * inverse[:, column : column + 1]
        combined = total + features[pl.ds(start + i * size, size), :].astype(jnp.float32)
        result = jnp.dot(combined.astype(jnp.bfloat16), weight[...], preferred_element_type=jnp.float32)
        done[here, :] = jnp.maximum(result, 0.0).astype(done.dtype)
    copy = pltpu.make_async_copy(done, out.at[rows], sem)
    copy.start()
    copy.wait()


def finish(part, mine, other, degrees, features, weight, before=None):
    args = [mine, other, degrees, features, weight] + ([] if before is None else [before])
    return pl.pallas_call(
        functools.partial(finish_kernel, part * mine.shape[0]),
        out_shape=jax.ShapeDtypeStruct(features.shape, jnp.bfloat16),
        in_specs=[VMEM] * 5 + [HBM] * (len(args) - 5),
        out_specs=HBM,
        scratch_shapes=[pltpu.VMEM(mine.shape, jnp.bfloat16), pltpu.SemaphoreType.DMA],
        input_output_aliases={} if before is None else {5: 0},
        compiler_params=pltpu.CompilerParams(vmem_limit_bytes=12 * 2**20),
        cost_estimate=pl.CostEstimate(
            flops=2 * mine.size * weight.shape[1], bytes_accessed=mine.size * 12, transcendentals=0
        ),
    )(*args)


def on_device(features, degrees, weight, tile_values, tile_pos, live):
    scatter, spread, gather, trade = plan()
    swap = [(i, i ^ 1) for i in range(len(CHIPS) * CORES)]
    send = lambda x, pairs: lax.ppermute(x, AXES, pairs)
    height, width = features.shape
    blocks, half, tile = tile_values.shape[1:4]
    side = height // tile
    core = lax.axis_index("rep")
    me = lax.axis_index("rows") * CORES + core
    fact = lax.dynamic_index_in_dim(jnp.asarray(facts()), me, 0, keepdims=False)
    order = fact[5:]

    own = tile_values[0]
    peer = send(own, swap)
    own = pltpu.with_memory_space_constraint(own, pltpu.HBM)

    degrees = degrees.reshape(-1, 128)
    in_hbm = lambda x: pltpu.with_memory_space_constraint(x, pltpu.HBM)
    cut = pl.pallas_call(
        functools.partial(scale_kernel, blocks),
        out_shape=[jax.ShapeDtypeStruct((height // PIECES, width), jnp.bfloat16)] * PIECES,
        in_specs=[HBM, HBM],
        out_specs=[VMEM] * PIECES,
        scratch_shapes=[
            pltpu.VMEM(features.shape, features.dtype),
            pltpu.VMEM(degrees.shape, degrees.dtype),
            pltpu.SemaphoreType.DMA((2,)),
        ],
        compiler_params=pltpu.CompilerParams(vmem_limit_bytes=4 * 2**20),
    )(in_hbm(features), in_hbm(degrees))

    used = jnp.arange(half * CORES)[None, :] < live[0][:, None]
    row = jnp.where(used, tile_pos[0] // side * tile, -1)
    column = tile_pos[0] % side * tile
    both = jnp.stack([row, column]).reshape(2, blocks, CORES, half)
    table = jnp.where(core == 0, both, both[:, :, ::-1]).reshape(-1)

    piece = jnp.where(fact[0] == 1, cut[0], jnp.zeros_like(cut[0]))
    for got in [send(cut[i], pairs) for i, pairs in enumerate(scatter)]:
        piece = piece + got
    kept = piece
    for got in [send(kept, pairs) for pairs in spread]:
        piece = piece + got
    pieces = [piece] + [send(piece, pairs) for pairs in gather]
    source = pl.pallas_call(
        assemble_kernel,
        out_shape=jax.ShapeDtypeStruct((height, width), features.dtype),
        in_specs=[SMEM] + [VMEM] * 4,
        out_specs=VMEM,
        compiler_params=pltpu.CompilerParams(vmem_limit_bytes=4 * 2**20),
    )(fact[1:5], *pieces)
    order, source = lax.optimization_barrier((order, source))
    traded = [send(source, pairs) for pairs in trade]
    matrix = jax.ShapeDtypeStruct((height, height), own.dtype)
    mats = pl.pallas_call(
        prepare_kernel,
        out_shape=[matrix] * COLORS,
        in_specs=[SMEM, SMEM, HBM, HBM],
        out_specs=[VMEM] * COLORS,
        scratch_shapes=[pltpu.SemaphoreType.DMA((COLORS,))],
        compiler_params=pltpu.CompilerParams(vmem_limit_bytes=24 * 2**20),
        cost_estimate=pl.CostEstimate(flops=0, bytes_accessed=own.size * 4, transcendentals=0),
    )(order, table, own, peer)
    total = None
    for mat, block in zip(mats[:-1], [source] + traded[:-1]):
        total = multiply(mat, block, total)
    parts = [multiply(mats[-1], traded[-1], total, part) for part in range(2)]
    others = [send(part, swap) for part in parts]
    result = finish(0, parts[0], others[0], degrees, features, weight)
    return finish(1, parts[1], others[1], degrees, features, weight, result)


def solution(mesh):
    placed = (
        P("rows", None),
        P("rows"),
        P(),
        P("rows", None, "rep", None, None),
        P("rows", None, None),
        P("rows", None),
    )
    return jax.shard_map(on_device, mesh=mesh, in_specs=placed, out_specs=P("rows", None), check_vma=False)
```

```python
import functools
import itertools

import jax
import jax.numpy as jnp
import numpy as np
from jax import lax
from jax.experimental import pallas as pl
from jax.experimental.pallas import tpu as pltpu
from jax.sharding import PartitionSpec as P

NZ, NX, NY, CORES = 8, 4, 4, 2
AXES = ("rows", "rep")
CHIPS = list(itertools.product(range(NZ), range(NX), range(NY)))
COLORS = 4
PIECES = 4
SIGNS = ((1, 1), (1, -1), (-1, 1), (-1, -1))
HOLDERS = (
    ((0, 0), (2, 1), (0, 3), (6, 1), (1, 3), (3, 0), (6, 3), (4, 3)),
    ((0, 2), (3, 2), (5, 2), (1, 1), (0, 1), (4, 1), (5, 1), (2, 2)),
    ((7, 3), (5, 0), (7, 1), (6, 2), (2, 3), (2, 0), (4, 2), (4, 0)),
    ((7, 0), (7, 2), (6, 0), (5, 3), (1, 0), (3, 1), (3, 3), (1, 2)),
)
GROUP_SHIFT = 1
PARTNERS = 1


def flat(z, x, y, core):
    return ((z % NZ * NX + x % NX) * NY + y % NY) * CORES + core


def color_of(z, x, y, core):
    return (z + 2 * x - y if core == 0 else z + 2 * y - x) % COLORS


def chip_at(color, height, across, core):
    up, side = SIGNS[color]
    height, across = up * height % NZ, side * across % NX
    z, other = color + COLORS * core + height, height + 2 * across
    return (z, across, other) if core == 0 else (z, other, across)


def partner(height, across, i):
    if i & 1:
        height = (height - GROUP_SHIFT ^ 1) + GROUP_SHIFT
    return height % NZ, across ^ (PARTNERS if i & 2 else 0)


def plan():
    scatter = [[] for _ in range(PIECES)]
    spread, gather, trade = ([[] for _ in range(3)] for _ in range(3))
    for color, core in itertools.product(range(COLORS), range(CORES)):
        at = lambda place, on=core: flat(*chip_at(color, *place, core), on)
        owner = (0, 0)
        for piece, places in enumerate(HOLDERS):
            if places[0] != owner:
                scatter[piece].append((at(owner), at(places[0])))
                scatter[piece].append((at(owner, 1 - core), at(places[4])))
            else:
                scatter[piece].append((at(owner), at(places[4])))
            for holder in (0, 4):
                for i in range(3):
                    spread[i].append((at(places[holder]), at(places[holder + 1 + i])))
        for place in itertools.product(range(NZ), range(NX)):
            for i in range(1, 4):
                gather[i - 1].append((at(partner(*place, i)), at(place)))
    for z, x, y in CHIPS:
        for core, s in ((0, 1), (1, -1)):
            for i, (dz, dx, dy) in enumerate(((1, 0, 0), (0, 1, 0), (0, 0, 1))):
                trade[i].append((flat(z, x, y, core), flat(z + s * dz, x + s * dx, y + s * dy, core)))
    return scatter, spread, gather, trade


def facts():
    rows = []
    for z, x, y in CHIPS:
        for core, s in ((0, 1), (1, -1)):
            color = color_of(z, x, y, core)
            up, side = SIGNS[color]
            place = up * (z - color - COLORS * core) % NZ, side * (x, y)[core] % NX
            row = [int(place == (0, 0))]
            for i in range(4):
                row.append(next(p for p, places in enumerate(HOLDERS) if partner(*place, i) in places))
            sent = [color_of(z - s, x, y, core), color_of(z, x - s, y, core), color_of(z, x, y - s, core)]
            row += [c + COLORS * core for c in [color] + sent]
            rows.append(row)
    return np.array(rows, np.int32)


VMEM = pl.BlockSpec(memory_space=pltpu.VMEM)
SMEM = pl.BlockSpec(memory_space=pltpu.SMEM)
HBM = pl.BlockSpec(memory_space=pltpu.HBM)


def inverse_columns(degrees):
    groups, lanes = degrees.shape
    padded = jnp.concatenate([degrees[...], jnp.ones((-groups % 8, lanes), degrees.dtype)], axis=0)
    return lax.rsqrt(padded.astype(jnp.float32)).T


def scale_kernel(blocks, features, degrees, *refs):
    *outs, held, held_degrees, sems = refs

    @pl.when(lax.axis_index("rows") % (lax.axis_size("rows") // blocks) == 0)
    def _():
        copies = [
            pltpu.make_async_copy(degrees, held_degrees, sems.at[0]),
            pltpu.make_async_copy(features, held, sems.at[1]),
        ]
        for copy in copies:
            copy.start()
        copies[0].wait()
        inverse = inverse_columns(held_degrees)
        copies[1].wait()
        groups, size = degrees.shape
        for i in range(groups):
            out, place = outs[i * len(outs) // groups], i % (groups // len(outs)) * size
            here = held[pl.ds(i * size, size), :].astype(jnp.float32)
            out[pl.ds(place, size), :] = (here * inverse[:, i : i + 1]).astype(out.dtype)


def assemble_kernel(slots, *refs):
    *pieces, out = refs
    size = pieces[0].shape[0]
    for i, piece in enumerate(pieces):
        out[pl.ds(pl.multiple_of(slots[i] * size, size), size), :] = piece[...]


def prepare_kernel(order, table, own, peer, *refs):
    *mats, sems = refs
    blocks, half, tile = own.shape[:3]
    slots = CORES * half
    places = [(j, k) for j in range(len(mats)) for k in range(slots)]

    def place(j, k, act):
        entry = order[j] * slots + k
        row, column = table[entry], table[blocks * slots + entry]

        @pl.when(row >= 0)
        def _():
            target = mats[j].at[pl.ds(pl.multiple_of(row, tile), tile), pl.ds(pl.multiple_of(column, tile), tile)]
            act(pltpu.make_async_copy((own if k < half else peer).at[order[j], k % half], target, sems.at[j]))

    for j, k in places:
        if k == 0:
            mats[j][...] = jnp.zeros(mats[j].shape, mats[j].dtype)
        place(j, k, lambda copy: copy.start())
    for j, k in places:
        place(j, k, lambda copy: copy.wait())


def multiply_kernel(mat, source, *refs):
    *before, out = refs
    product = jnp.dot(mat[...], source[...], preferred_element_type=jnp.float32)
    out[...] = before[0][...] + product if before else product


def multiply_part_kernel(start, mat, source, before, out):
    rows = pl.ds(start, out.shape[0])
    out[...] = before[rows, :] + jnp.dot(mat[rows, :], source[...], preferred_element_type=jnp.float32)


def multiply(mat, source, before=None, part=None):
    args = [mat, source] + ([] if before is None else [before])
    height, width = source.shape
    if part is None:
        kernel, alias = multiply_kernel, ({} if before is None else {2: 0})
    else:
        height //= 2
        kernel, alias = functools.partial(multiply_part_kernel, part * height), {}
    return pl.pallas_call(
        kernel,
        out_shape=jax.ShapeDtypeStruct((height, width), jnp.float32),
        in_specs=[VMEM] * len(args),
        out_specs=VMEM,
        input_output_aliases=alias,
        compiler_params=pltpu.CompilerParams(vmem_limit_bytes=10 * 2**20),
        cost_estimate=pl.CostEstimate(
            flops=2 * height * mat.shape[1] * width, bytes_accessed=mat.size * 2, transcendentals=0
        ),
    )(*args)


def finish_rows(i, start, mine, other, inverse, features, weight, done):
    size = inverse.shape[0]
    here = pl.ds(i * size, size)
    column = start // size + i
    total = (mine[here, :] + other[here, :]) * inverse[:, column : column + 1]
    combined = total + features[pl.ds(start + i * size, size), :].astype(jnp.float32)
    result = jnp.dot(combined.astype(jnp.bfloat16), weight[...], preferred_element_type=jnp.float32)
    done[here, :] = jnp.maximum(result, 0.0).astype(done.dtype)


def finish_first_kernel(mine, other, degrees, features, weight, done):
    inverse = inverse_columns(degrees)
    for i in range(mine.shape[0] // inverse.shape[0]):
        finish_rows(i, 0, mine, other, inverse, features, weight, done)


def finish_second_kernel(mine, other, degrees, features, weight, first, out, done, sems):
    half, size = mine.shape[0], degrees.shape[1]
    copies = [pltpu.make_async_copy(first, out.at[pl.ds(0, half)], sems.at[half // size])]
    copies[0].start()
    inverse = inverse_columns(degrees)
    for i in range(half // size):
        finish_rows(i, half, mine, other, inverse, features, weight, done)
        group = done.at[pl.ds(i * size, size)]
        copies.append(pltpu.make_async_copy(group, out.at[pl.ds(half + i * size, size)], sems.at[i]))
        copies[-1].start()
    for copy in copies:
        copy.wait()


def finish(mine, other, degrees, features, weight, first=None):
    half = jax.ShapeDtypeStruct(mine.shape, jnp.bfloat16)
    last = first is not None
    args = [mine, other, degrees, features, weight] + ([first] if last else [])
    return pl.pallas_call(
        finish_second_kernel if last else finish_first_kernel,
        out_shape=jax.ShapeDtypeStruct(features.shape, jnp.bfloat16) if last else half,
        in_specs=[VMEM] * len(args),
        out_specs=HBM if last else VMEM,
        scratch_shapes=[
            pltpu.VMEM(half.shape, half.dtype),
            pltpu.SemaphoreType.DMA((mine.shape[0] // degrees.shape[1] + 1,)),
        ]
        if last
        else [],
        compiler_params=pltpu.CompilerParams(vmem_limit_bytes=12 * 2**20),
        cost_estimate=pl.CostEstimate(
            flops=2 * mine.size * weight.shape[1], bytes_accessed=mine.size * 12, transcendentals=0
        ),
    )(*args)


def on_device(features, degrees, weight, tile_values, tile_pos, live):
    scatter, spread, gather, trade = plan()
    swap = [(i, i ^ 1) for i in range(len(CHIPS) * CORES)]
    send = lambda x, pairs: lax.ppermute(x, AXES, pairs)
    height, width = features.shape
    blocks, half, tile = tile_values.shape[1:4]
    side = height // tile
    core = lax.axis_index("rep")
    me = lax.axis_index("rows") * CORES + core
    fact = lax.dynamic_index_in_dim(jnp.asarray(facts()), me, 0, keepdims=False)
    order = fact[5:]

    own = tile_values[0]
    peer = send(own, swap)
    own = pltpu.with_memory_space_constraint(own, pltpu.HBM)

    degrees = degrees.reshape(-1, 128)
    in_hbm = lambda x: pltpu.with_memory_space_constraint(x, pltpu.HBM)
    cut = pl.pallas_call(
        functools.partial(scale_kernel, blocks),
        out_shape=[jax.ShapeDtypeStruct((height // PIECES, width), jnp.bfloat16)] * PIECES,
        in_specs=[HBM, HBM],
        out_specs=[VMEM] * PIECES,
        scratch_shapes=[
            pltpu.VMEM(features.shape, features.dtype),
            pltpu.VMEM(degrees.shape, degrees.dtype),
            pltpu.SemaphoreType.DMA((2,)),
        ],
        compiler_params=pltpu.CompilerParams(vmem_limit_bytes=4 * 2**20),
    )(in_hbm(features), in_hbm(degrees))

    used = jnp.arange(half * CORES)[None, :] < live[0][:, None]
    row = jnp.where(used, tile_pos[0] // side * tile, -1)
    column = tile_pos[0] % side * tile
    both = jnp.stack([row, column]).reshape(2, blocks, CORES, half)
    table = jnp.where(core == 0, both, both[:, :, ::-1]).reshape(-1)

    piece = jnp.where(fact[0] == 1, cut[0], jnp.zeros_like(cut[0]))
    for got in [send(cut[i], pairs) for i, pairs in enumerate(scatter)]:
        piece = piece + got
    table, kept = lax.optimization_barrier((table, piece))
    for got in [send(kept, pairs) for pairs in spread]:
        piece = piece + got
    pieces = [piece] + [send(piece, pairs) for pairs in gather]
    source = pl.pallas_call(
        assemble_kernel,
        out_shape=jax.ShapeDtypeStruct((height, width), features.dtype),
        in_specs=[SMEM] + [VMEM] * 4,
        out_specs=VMEM,
        compiler_params=pltpu.CompilerParams(vmem_limit_bytes=4 * 2**20),
    )(fact[1:5], *pieces)
    order, source = lax.optimization_barrier((order, source))
    traded = [send(source, pairs) for pairs in trade]
    matrix = jax.ShapeDtypeStruct((height, height), own.dtype)
    mats = pl.pallas_call(
        prepare_kernel,
        out_shape=[matrix] * COLORS,
        in_specs=[SMEM, SMEM, HBM, HBM],
        out_specs=[VMEM] * COLORS,
        scratch_shapes=[pltpu.SemaphoreType.DMA((COLORS,))],
        compiler_params=pltpu.CompilerParams(vmem_limit_bytes=24 * 2**20),
        cost_estimate=pl.CostEstimate(flops=0, bytes_accessed=own.size * 4, transcendentals=0),
    )(order, table, own, peer)
    total = None
    for mat, block in zip(mats[:-1], [source] + traded[:-1]):
        total = multiply(mat, block, total)
    parts = [multiply(mats[-1], traded[-1], total, part) for part in range(2)]
    others = [send(part, swap) for part in parts]
    result = finish(parts[0], others[0], degrees, features, weight)
    return finish(parts[1], others[1], degrees, features, weight, result)


def solution(mesh):
    placed = (
        P("rows", None),
        P("rows"),
        P(),
        P("rows", None, "rep", None, None),
        P("rows", None, None),
        P("rows", None),
    )
    return jax.shard_map(on_device, mesh=mesh, in_specs=placed, out_specs=P("rows", None), check_vma=False)
```

```python
import functools
import itertools

import jax
import jax.numpy as jnp
import numpy as np
from jax import lax
from jax.experimental import pallas as pl
from jax.experimental.pallas import tpu as pltpu
from jax.sharding import PartitionSpec as P

NZ, NX, NY, CORES = 8, 4, 4, 2
AXES = ("rows", "rep")
CHIPS = list(itertools.product(range(NZ), range(NX), range(NY)))
COLORS = 4
PIECES = 4
SIGNS = ((1, 1), (1, -1), (-1, 1), (-1, -1))
HOLDERS = (
    ((0, 0), (2, 1), (0, 3), (6, 1), (1, 3), (3, 0), (6, 3), (4, 3)),
    ((0, 2), (3, 2), (5, 2), (1, 1), (0, 1), (4, 1), (5, 1), (2, 2)),
    ((7, 3), (5, 0), (7, 1), (6, 2), (2, 3), (2, 0), (4, 2), (4, 0)),
    ((7, 0), (7, 2), (6, 0), (5, 3), (1, 0), (3, 1), (3, 3), (1, 2)),
)
GROUP_SHIFT = 1
PARTNERS = 1


def flat(z, x, y, core):
    return ((z % NZ * NX + x % NX) * NY + y % NY) * CORES + core


def color_of(z, x, y, core):
    return (z + 2 * x - y if core == 0 else z + 2 * y - x) % COLORS


def chip_at(color, height, across, core):
    up, side = SIGNS[color]
    height, across = up * height % NZ, side * across % NX
    z, other = color + COLORS * core + height, height + 2 * across
    return (z, across, other) if core == 0 else (z, other, across)


def partner(height, across, i):
    if i & 1:
        height = (height - GROUP_SHIFT ^ 1) + GROUP_SHIFT
    return height % NZ, across ^ (PARTNERS if i & 2 else 0)


def plan():
    scatter = [[] for _ in range(PIECES)]
    spread, gather, trade = ([[] for _ in range(3)] for _ in range(3))
    for color, core in itertools.product(range(COLORS), range(CORES)):
        at = lambda place, on=core: flat(*chip_at(color, *place, core), on)
        owner = (0, 0)
        for piece, places in enumerate(HOLDERS):
            if places[0] != owner:
                scatter[piece].append((at(owner), at(places[0])))
                scatter[piece].append((at(owner, 1 - core), at(places[4])))
            else:
                scatter[piece].append((at(owner), at(places[4])))
            for holder in (0, 4):
                for i in range(3):
                    spread[i].append((at(places[holder]), at(places[holder + 1 + i])))
        for place in itertools.product(range(NZ), range(NX)):
            for i in range(1, 4):
                gather[i - 1].append((at(partner(*place, i)), at(place)))
    for z, x, y in CHIPS:
        for core, s in ((0, 1), (1, -1)):
            for i, (dz, dx, dy) in enumerate(((1, 0, 0), (0, 1, 0), (0, 0, 1))):
                trade[i].append((flat(z, x, y, core), flat(z + s * dz, x + s * dx, y + s * dy, core)))
    return scatter, spread, gather, trade


def facts():
    rows = []
    for z, x, y in CHIPS:
        for core, s in ((0, 1), (1, -1)):
            color = color_of(z, x, y, core)
            up, side = SIGNS[color]
            place = up * (z - color - COLORS * core) % NZ, side * (x, y)[core] % NX
            row = [int(place == (0, 0))]
            for i in range(4):
                row.append(next(p for p, places in enumerate(HOLDERS) if partner(*place, i) in places))
            sent = [color_of(z - s, x, y, core), color_of(z, x - s, y, core), color_of(z, x, y - s, core)]
            row += [c + COLORS * core for c in [color] + sent]
            rows.append(row)
    return np.array(rows, np.int32)


VMEM = pl.BlockSpec(memory_space=pltpu.VMEM)
SMEM = pl.BlockSpec(memory_space=pltpu.SMEM)
HBM = pl.BlockSpec(memory_space=pltpu.HBM)


def inverse_columns(degrees):
    groups, lanes = degrees.shape
    padded = jnp.concatenate([degrees[...], jnp.ones((-groups % 8, lanes), degrees.dtype)], axis=0)
    return lax.rsqrt(padded.astype(jnp.float32)).T


def scale_kernel(blocks, features, degrees, *refs):
    *outs, held, held_degrees, sems = refs

    @pl.when(lax.axis_index("rows") % (lax.axis_size("rows") // blocks) == 0)
    def _():
        copies = [
            pltpu.make_async_copy(degrees, held_degrees, sems.at[0]),
            pltpu.make_async_copy(features, held, sems.at[1]),
        ]
        for copy in copies:
            copy.start()
        copies[0].wait()
        inverse = inverse_columns(held_degrees)
        copies[1].wait()
        groups, size = degrees.shape
        for i in range(groups):
            out, place = outs[i * len(outs) // groups], i % (groups // len(outs)) * size
            here = held[pl.ds(i * size, size), :].astype(jnp.float32)
            out[pl.ds(place, size), :] = (here * inverse[:, i : i + 1]).astype(out.dtype)


def assemble_kernel(slots, *refs):
    *pieces, out = refs
    size = pieces[0].shape[0]
    for i, piece in enumerate(pieces):
        out[pl.ds(pl.multiple_of(slots[i] * size, size), size), :] = piece[...]


def prepare_kernel(order, table, own, peer, *refs):
    *mats, sems = refs
    blocks, half, tile = own.shape[:3]
    slots = CORES * half
    places = [(j, k) for j in range(len(mats)) for k in range(slots)]

    def place(j, k, act):
        entry = order[j] * slots + k
        row, column = table[entry], table[blocks * slots + entry]

        @pl.when(row >= 0)
        def _():
            target = mats[j].at[pl.ds(pl.multiple_of(row, tile), tile), pl.ds(pl.multiple_of(column, tile), tile)]
            act(pltpu.make_async_copy((own if k < half else peer).at[order[j], k % half], target, sems.at[j]))

    for j, k in places:
        if k == 0:
            mats[j][...] = jnp.zeros(mats[j].shape, mats[j].dtype)
        place(j, k, lambda copy: copy.start())
    for j, k in places:
        place(j, k, lambda copy: copy.wait())


def multiply_kernel(mat, source, *refs):
    *before, out = refs
    product = jnp.dot(mat[...], source[...], preferred_element_type=jnp.float32)
    out[...] = before[0][...] + product if before else product


def multiply_part_kernel(start, mat, source, before, out):
    rows = pl.ds(start, out.shape[0])
    out[...] = before[rows, :] + jnp.dot(mat[rows, :], source[...], preferred_element_type=jnp.float32)


def multiply(mat, source, before=None, part=None):
    args = [mat, source] + ([] if before is None else [before])
    height, width = source.shape
    if part is None:
        kernel, alias = multiply_kernel, ({} if before is None else {2: 0})
    else:
        start = part * (height * 2 // 3)
        height = height // 3 if part else height * 2 // 3
        kernel, alias = functools.partial(multiply_part_kernel, start), {}
    return pl.pallas_call(
        kernel,
        out_shape=jax.ShapeDtypeStruct((height, width), jnp.float32),
        in_specs=[VMEM] * len(args),
        out_specs=VMEM,
        input_output_aliases=alias,
        compiler_params=pltpu.CompilerParams(vmem_limit_bytes=10 * 2**20),
        cost_estimate=pl.CostEstimate(
            flops=2 * height * mat.shape[1] * width, bytes_accessed=mat.size * 2, transcendentals=0
        ),
    )(*args)


def finish_rows(i, start, mine, other, inverse, features, weight, done):
    size = inverse.shape[0]
    here = pl.ds(i * size, size)
    column = start // size + i
    total = (mine[here, :] + other[here, :]) * inverse[:, column : column + 1]
    combined = total + features[pl.ds(start + i * size, size), :].astype(jnp.float32)
    result = jnp.dot(combined.astype(jnp.bfloat16), weight[...], preferred_element_type=jnp.float32)
    done[here, :] = jnp.maximum(result, 0.0).astype(done.dtype)


def finish_first_kernel(mine, other, degrees, features, weight, done):
    inverse = inverse_columns(degrees)
    for i in range(mine.shape[0] // inverse.shape[0]):
        finish_rows(i, 0, mine, other, inverse, features, weight, done)


def finish_second_kernel(mine, other, degrees, features, weight, first, out, done, sems):
    start, rows, size = first.shape[0], mine.shape[0], degrees.shape[1]
    copies = [pltpu.make_async_copy(first, out.at[pl.ds(0, start)], sems.at[rows // size])]
    copies[0].start()
    inverse = inverse_columns(degrees)
    for i in range(rows // size):
        finish_rows(i, start, mine, other, inverse, features, weight, done)
        group = done.at[pl.ds(i * size, size)]
        copies.append(pltpu.make_async_copy(group, out.at[pl.ds(start + i * size, size)], sems.at[i]))
        copies[-1].start()
    for copy in copies:
        copy.wait()


def finish(mine, other, degrees, features, weight, first=None):
    half = jax.ShapeDtypeStruct(mine.shape, jnp.bfloat16)
    last = first is not None
    args = [mine, other, degrees, features, weight] + ([first] if last else [])
    return pl.pallas_call(
        finish_second_kernel if last else finish_first_kernel,
        out_shape=jax.ShapeDtypeStruct(features.shape, jnp.bfloat16) if last else half,
        in_specs=[VMEM] * len(args),
        out_specs=HBM if last else VMEM,
        scratch_shapes=[
            pltpu.VMEM(half.shape, half.dtype),
            pltpu.SemaphoreType.DMA((mine.shape[0] // degrees.shape[1] + 1,)),
        ]
        if last
        else [],
        compiler_params=pltpu.CompilerParams(vmem_limit_bytes=12 * 2**20),
        cost_estimate=pl.CostEstimate(
            flops=2 * mine.size * weight.shape[1], bytes_accessed=mine.size * 12, transcendentals=0
        ),
    )(*args)


def on_device(features, degrees, weight, tile_values, tile_pos, live):
    scatter, spread, gather, trade = plan()
    swap = [(i, i ^ 1) for i in range(len(CHIPS) * CORES)]
    send = lambda x, pairs: lax.ppermute(x, AXES, pairs)
    height, width = features.shape
    blocks, half, tile = tile_values.shape[1:4]
    side = height // tile
    core = lax.axis_index("rep")
    me = lax.axis_index("rows") * CORES + core
    fact = lax.dynamic_index_in_dim(jnp.asarray(facts()), me, 0, keepdims=False)
    order = fact[5:]

    own = tile_values[0]
    peer = send(own, swap)
    own = pltpu.with_memory_space_constraint(own, pltpu.HBM)

    degrees = degrees.reshape(-1, 128)
    in_hbm = lambda x: pltpu.with_memory_space_constraint(x, pltpu.HBM)
    cut = pl.pallas_call(
        functools.partial(scale_kernel, blocks),
        out_shape=[jax.ShapeDtypeStruct((height // PIECES, width), jnp.bfloat16)] * PIECES,
        in_specs=[HBM, HBM],
        out_specs=[VMEM] * PIECES,
        scratch_shapes=[
            pltpu.VMEM(features.shape, features.dtype),
            pltpu.VMEM(degrees.shape, degrees.dtype),
            pltpu.SemaphoreType.DMA((2,)),
        ],
        compiler_params=pltpu.CompilerParams(vmem_limit_bytes=4 * 2**20),
    )(in_hbm(features), in_hbm(degrees))

    used = jnp.arange(half * CORES)[None, :] < live[0][:, None]
    row = jnp.where(used, tile_pos[0] // side * tile, -1)
    column = tile_pos[0] % side * tile
    both = jnp.stack([row, column]).reshape(2, blocks, CORES, half)
    table = jnp.where(core == 0, both, both[:, :, ::-1]).reshape(-1)

    piece = jnp.where(fact[0] == 1, cut[0], jnp.zeros_like(cut[0]))
    for got in [send(cut[i], pairs) for i, pairs in enumerate(scatter)]:
        piece = piece + got
    table, kept = lax.optimization_barrier((table, piece))
    for got in [send(kept, pairs) for pairs in spread]:
        piece = piece + got
    pieces = [piece] + [send(piece, pairs) for pairs in gather]
    source = pl.pallas_call(
        assemble_kernel,
        out_shape=jax.ShapeDtypeStruct((height, width), features.dtype),
        in_specs=[SMEM] + [VMEM] * 4,
        out_specs=VMEM,
        compiler_params=pltpu.CompilerParams(vmem_limit_bytes=4 * 2**20),
    )(fact[1:5], *pieces)
    order, source = lax.optimization_barrier((order, source))
    traded = [send(source, pairs) for pairs in trade]
    matrix = jax.ShapeDtypeStruct((height, height), own.dtype)
    mats = pl.pallas_call(
        prepare_kernel,
        out_shape=[matrix] * COLORS,
        in_specs=[SMEM, SMEM, HBM, HBM],
        out_specs=[VMEM] * COLORS,
        scratch_shapes=[pltpu.SemaphoreType.DMA((COLORS,))],
        compiler_params=pltpu.CompilerParams(vmem_limit_bytes=24 * 2**20),
        cost_estimate=pl.CostEstimate(flops=0, bytes_accessed=own.size * 4, transcendentals=0),
    )(order, table, own, peer)
    total = None
    for mat, block in zip(mats[:-1], [source] + traded[:-1]):
        total = multiply(mat, block, total)
    parts = [multiply(mats[-1], traded[-1], total, part) for part in range(2)]
    others = [send(part, swap) for part in parts]
    result = finish(parts[0], others[0], degrees, features, weight)
    return finish(parts[1], others[1], degrees, features, weight, result)


def solution(mesh):
    placed = (
        P("rows", None),
        P("rows"),
        P(),
        P("rows", None, "rep", None, None),
        P("rows", None, None),
        P("rows", None),
    )
    return jax.shard_map(on_device, mesh=mesh, in_specs=placed, out_specs=P("rows", None), check_vma=False)
```
